256 devices in a mesh: dp: 8 (over x, z_lo), segment: 32 (over y, z_hi, core).
Axes of the slice: x: 4, y: 4, z: 8 (z_hi: 4, z_lo: 2; z = z_hi * 2 + z_lo), core: 2. Of those that a mesh axis runs over, the one named last changes fastest.
Arguments:
- feed_rising: bfloat16 [4, 512, 512], P(None, 'dp'), may hold values from -6 to 6
- feed_falling: bfloat16 [4, 512, 512], P(None, 'dp'), may hold values from -6 to 6
- up_weight: bfloat16 [64, 512, 1024], P('segment'), as said below
- down_weight: bfloat16 [64, 1024, 512], P('segment'), as said below
- norm_gain: float32 [64, 512], P('segment'), as said below
Outputs:
- grad_up: float32 [512, 16384], P('dp', 'segment')
- grad_down: float32 [16384, 512], P('segment', 'dp')
- grad_gain: float32 [32, 256], P('segment', 'dp')
The draws below stay inside these ranges and needn't reach their ends.
Inputs may be any that keep to these rules, and one draw needn't show every extreme that they name: `up_weight`: normal entries of standard deviation 512^-0.5; the rows of one section (2i, 2i + 1 as in the meaning) are equal. `down_weight`: normal entries of standard deviation 1024^-0.5; the rows of one section are equal. `norm_gain`: the rows of one section are equal.
All inputs are finite; a program needn't handle non-finite values.
Results may differ from the reference program's by a relative error of at most 0.011.
Values may be sent and summed in bfloat16 or wider, within the bound.
No kernel may reach another device: no remote copies, remote signals or barrier semaphores. Data moves between devices by JAX's collectives and lax.ppermute only.
A program may use at most 64 MiB of HBM per device.

```python
import math
import jax
import jax.numpy as jnp
from jax import lax

D = 512
H = 1024
M = 4
ROWS_DEV = 32
SECTIONS = 16
MB_ROWS = 512


def section_rows(base):
    order = jnp.arange(4 * SECTIONS)
    device = order // 2
    picked = jnp.where(order % 2 == 0, device // 2, SECTIONS - 1 - device // 2)
    return base[picked]


def draw_up_weight(key, part):
    key = jax.random.fold_in(key, 11)
    base = jax.random.normal(key, (SECTIONS, D, H), jnp.float32) * D ** (-0.5)
    return section_rows(base).astype(jnp.bfloat16)


def draw_down_weight(key, part):
    key = jax.random.fold_in(key, 23)
    base = jax.random.normal(key, (SECTIONS, H, D), jnp.float32) * H ** (-0.5)
    return section_rows(base).astype(jnp.bfloat16)


def draw_norm_gain(key, part):
    key = jax.random.fold_in(key, 37)
    base = jax.random.uniform(key, (SECTIONS, D), jnp.float32, 0.5, 1.5)
    return section_rows(base)


def steps_of(stream_key, shape, cuts, least, high):
    def one(position, shards_of):
        steps = jax.random.uniform(jax.random.fold_in(jax.random.fold_in(stream_key, 6), position), (shards_of,), jnp.float32, least / len(cuts), high / len(cuts))
        return jnp.repeat(jnp.exp(steps), shape[position] // shards_of).reshape((-1,) + (1,) * (len(shape) - position - 1))

    loudness = one(*cuts[0])
    for cut in cuts[1:]:
        loudness = loudness * one(*cut)
    return loudness


def gaussian(key, dims, scale, reach, cuts=(), dtype=jnp.bfloat16):
    entries = scale * jax.random.normal(key, dims, jnp.float32)
    if cuts:
        entries = entries * steps_of(key, dims, cuts, -0.22, 0.18)
    return jnp.clip(entries, -reach, reach).astype(dtype)


def setup_inputs(seed: int = 0) -> dict:
    keys = jax.random.split(jax.random.key(seed), 6)
    return {
        "feed_rising": gaussian(keys[0], (M, MB_ROWS, D), 1.0, 6.0, ((1, 8),)),
        "feed_falling": gaussian(keys[1], (M, MB_ROWS, D), 1.0, 6.0, ((1, 8),)),
        "up_weight": draw_up_weight(jax.random.fold_in(keys[5], 71), 0),
        "down_weight": draw_down_weight(jax.random.fold_in(keys[5], 71), 0),
        "norm_gain": draw_norm_gain(jax.random.fold_in(keys[5], 71), 0),
    }


GELU_C = 0.7978845608028654
CUBIC = 0.044715

def gelu_parts(pre_act):
    inner_arg = GELU_C * (pre_act + CUBIC * pre_act * pre_act * pre_act)
    tangent = jnp.tanh(inner_arg)
    gelu_value = 0.5 * pre_act * (1.0 + tangent)
    gelu_slope = 0.5 * (1.0 + tangent) + 0.5 * pre_act * (1.0 - tangent * tangent) * GELU_C * (1.0 + 3.0 * CUBIC * pre_act * pre_act)
    return (gelu_value, gelu_slope)

def norm_parts(activations, gain_row):
    values = activations.astype(jnp.float32)
    centre = lax.optimization_barrier(jnp.mean(values, axis=-1, keepdims=True))
    spread = lax.optimization_barrier(jnp.mean(jnp.square(values - centre), axis=-1, keepdims=True))
    inverse = lax.rsqrt(spread + 1e-05)
    normed = (values - centre) * inverse
    return (normed, inverse, (normed * gain_row).astype(jnp.bfloat16))

def block_sum(part):
    rounded = lax.optimization_barrier(part.astype(jnp.bfloat16))
    return lax.optimization_barrier(jnp.sum(rounded.astype(jnp.float32), axis=0))

def reference(feed_rising, feed_falling, up_weight, down_weight, norm_gain):
    up_sections = up_weight[::4].astype(jnp.float32)
    down_sections = down_weight[::4].astype(jnp.float32)
    gain_sections = norm_gain[::4]
    blocks = MB_ROWS // ROWS_DEV
    loss_scale = 1.0 / math.sqrt(2.0 * M * MB_ROWS)
    grad_u = [jnp.zeros((D, H), jnp.float32) for section in range(SECTIONS)]
    grad_w = [jnp.zeros((H, D), jnp.float32) for section in range(SECTIONS)]
    grad_g = [jnp.zeros((D,), jnp.float32) for section in range(SECTIONS)]
    for entering in (feed_rising, feed_falling):
        activations = entering
        stored_parts = []
        for section in range(SECTIONS):
            normed, inverse, normed_b = norm_parts(activations, gain_sections[section])
            pre_act = jnp.einsum('mrd,dh->mrh', normed_b.astype(jnp.float32), up_sections[section])
            gelu_value, gelu_slope = gelu_parts(pre_act)
            hidden = gelu_value.astype(jnp.bfloat16)
            emitted = activations.astype(jnp.float32) + jnp.einsum('mrh,hd->mrd', hidden.astype(jnp.float32), down_sections[section])
            stored_parts.append((normed, inverse, normed_b, gelu_slope, hidden))
            activations = emitted.astype(jnp.bfloat16)
        cotangent = (activations.astype(jnp.float32) * loss_scale).astype(jnp.bfloat16)
        for section in reversed(range(SECTIONS)):
            normed, inverse, normed_b, gelu_slope, hidden = stored_parts[section]
            cot_f = cotangent.astype(jnp.float32)
            back_hidden = jnp.einsum('mrd,hd->mrh', cot_f, down_sections[section])
            pre_grad = (back_hidden * gelu_slope).astype(jnp.bfloat16)
            pre_f = pre_grad.astype(jnp.float32)
            part_w = jnp.einsum('mbrh,mbrd->bhd', hidden.astype(jnp.float32).reshape(M, blocks, ROWS_DEV, H), cot_f.reshape(M, blocks, ROWS_DEV, D))
            grad_w[section] = grad_w[section] + block_sum(part_w)
            part_u = jnp.einsum('mbrd,mbrh->bdh', normed_b.astype(jnp.float32).reshape(M, blocks, ROWS_DEV, D), pre_f.reshape(M, blocks, ROWS_DEV, H))
            grad_u[section] = grad_u[section] + block_sum(part_u)
            back_norm = jnp.einsum('mrh,dh->mrd', pre_f, up_sections[section])
            part_g = lax.optimization_barrier(jnp.sum((back_norm * normed).reshape(M, blocks, ROWS_DEV, D), axis=(0, 2)))
            grad_g[section] = grad_g[section] + block_sum(part_g)
            scaled = back_norm * gain_sections[section]
            first_mean = lax.optimization_barrier(jnp.mean(scaled, axis=-1, keepdims=True))
            second_mean = lax.optimization_barrier(jnp.mean(scaled * normed, axis=-1, keepdims=True))
            cotangent = (cot_f + inverse * (scaled - first_mean - normed * second_mean)).astype(jnp.bfloat16)
    grad_up = jnp.stack(grad_u, axis=1).reshape(D, SECTIONS * H)
    grad_down = jnp.stack(grad_w, axis=0).reshape(SECTIONS * H, D)
    grad_gain = jnp.stack(grad_g, axis=0).reshape(2 * SECTIONS, D // 2)
    return (grad_up, grad_down, grad_gain)
```

```python
import math

import jax
import jax.numpy as jnp
from jax import lax
from jax.experimental import pallas as pl
from jax.experimental.pallas import tpu as pltpu
from jax.sharding import PartitionSpec as P

GELU_C = 0.7978845608028654
CUBIC = 0.044715
BF = jnp.bfloat16
F4 = jnp.float32
VMEM = pltpu.VMEM


def in_vmem(x):
    return pltpu.with_memory_space_constraint(x, VMEM)


def call(kernel, outs, ins, name, aliases=None, flops=0, plain=False, anywhere=False, scratch=()):
    space = pl.BlockSpec(memory_space=VMEM)
    if plain:
        shapes = [jax.ShapeDtypeStruct(s, d) for s, d in outs]
    else:
        shapes = [VMEM(s, d) for s, d in outs]
    return pl.pallas_call(
        kernel,
        out_shape=shapes,
        in_specs=[pl.BlockSpec(memory_space=pl.ANY) if anywhere else space] * len(ins),
        out_specs=[space] * len(outs),
        name=name,
        input_output_aliases=aliases or {},
        scratch_shapes=list(scratch),
        cost_estimate=pl.CostEstimate(flops=flops, bytes_accessed=1 << 16, transcendentals=0),
        compiler_params=pltpu.CompilerParams(vmem_limit_bytes=16 << 20),
    )(*[pltpu.with_memory_space_constraint(x, pltpu.HBM) if anywhere else in_vmem(x) for x in ins])


def where_am_i():
    place = lax.axis_index("segment")
    return place // 2, place % 2


def norm_of(values):
    centre = jnp.mean(values, axis=-1, keepdims=True)
    spread = values - centre
    inverse = lax.rsqrt(jnp.mean(spread * spread, axis=-1, keepdims=True) + 1e-05)
    return spread * inverse, inverse


def load_kernel(rising, falling, up, down, gain, rows, up_v, down_v, gain_v, sems):
    pair, core = where_am_i()
    count = rising.shape[0]
    size = rows.shape[0] // count
    part = pl.ds(pl.multiple_of(core * size, size), size)
    late = (pair >= 8).astype(jnp.int32)

    def weights(j, k):
        return [
            pltpu.make_async_copy(up.at[j], up_v.at[j], sems.at[k]),
            pltpu.make_async_copy(down.at[j], down_v.at[j], sems.at[k + 1]),
        ]

    def feed(source):
        return [
            pltpu.make_async_copy(source.at[m, part], rows.at[pl.ds(m * size, size)], sems.at[5 + m])
            for m in range(count)
        ]

    first = weights(late, 0)
    second = weights(1 - late, 2)
    gains = pltpu.make_async_copy(gain, gain_v, sems.at[4])

    @pl.when(pair < 8)
    def _():
        for copy in feed(rising):
            copy.start()

    @pl.when(pair >= 8)
    def _():
        for copy in feed(falling):
            copy.start()

    gains.start()
    for copy in first + second:
        copy.start()
    for copy in feed(rising):
        copy.wait()
    gains.wait()
    for copy in first + second:
        copy.wait()


def transpose_kernel(source, _, out, token):
    for j in range(2):
        out[j] = source[j].T
    token[...] = jnp.zeros_like(token)


def held(section):
    pair, _ = where_am_i()
    late = (pair >= 8).astype(jnp.int32)
    return (pair == section) | (pair == 15 - section), (late if section < 8 else 1 - late)


def forward_kernel(section, rows, up, down, gain, _, emitted):
    turn, j = held(section)

    @pl.when(turn)
    def _():
        values = rows[...].astype(F4)
        normed, _ = norm_of(values)
        normed_b = (normed * gain[pl.ds(j, 1), :]).astype(BF)
        a = jnp.dot(normed_b, up[j], preferred_element_type=F4)
        tangent = jnp.tanh(a * (GELU_C + GELU_C * CUBIC * a * a))
        hidden = (0.5 * a * (1.0 + tangent)).astype(BF)
        emitted[...] = (values + jnp.dot(hidden, down[j], preferred_element_type=F4)).astype(BF)


def keep_kernel(section, rows, up, gain, _y, _a, _b, _c, _d, _e, xh, inv, nb, slope, hid, token):
    turn, j = held(section)

    @pl.when(turn)
    def _():
        normed, inverse = norm_of(rows[...].astype(F4))
        normed_b = (normed * gain[pl.ds(j, 1), :]).astype(BF)
        a = jnp.dot(normed_b, up[j], preferred_element_type=F4)
        square = a * a
        tangent = jnp.tanh(a * (GELU_C + GELU_C * CUBIC * square))
        half = 0.5 * (1.0 + tangent)
        hid[...] = (a * half).astype(BF)
        slope[...] = half + 0.5 * a * (1.0 - tangent * tangent) * (
            GELU_C + 3.0 * GELU_C * CUBIC * square
        )
        xh[...] = normed
        inv[...] = jnp.broadcast_to(inverse, inv.shape)
        nb[...] = normed_b

    token[...] = jnp.zeros_like(token)


def backward_kernel(section, scale, cot, up_t, down_t, gain, xh, inv, slope, _t, _a, _b, _c, sent, da, dy, gsum):
    turn, j = held(section)

    @pl.when(turn)
    def _():
        dy_b = cot[...]
        if scale is not None:
            dy_b = (dy_b.astype(F4) * scale).astype(BF)
        dp = jnp.dot(dy_b, down_t[j], preferred_element_type=F4)
        da_b = (dp * slope[...]).astype(BF)
        dn = jnp.dot(da_b, up_t[j], preferred_element_type=F4)
        normed = xh[...]
        e = dn * gain[pl.ds(j, 1), :]
        first = jnp.mean(e, axis=-1, keepdims=True)
        second = jnp.mean(e * normed, axis=-1, keepdims=True)
        sent[...] = (dy_b.astype(F4) + inv[:, :1] * (e - first - normed * second)).astype(BF)
        da[...] = da_b
        dy[...] = dy_b
        prod = dn * normed
        gsum[...] = jnp.sum(prod.reshape(prod.shape[0] // 8, 8, prod.shape[1]), axis=0)


def grads_kernel(nb, da, dy, hid, gsum, _, keep, give, token):
    _, core = where_am_i()
    dims = (((0,), (0,)), ((), ()))
    gains = jnp.sum(gsum[...], axis=0, keepdims=True)
    for which, out in ((core, keep), (1 - core, give)):
        cols = pl.ds(pl.multiple_of(which * 512, 512), 512)
        part_up = lax.dot_general(nb[...], da[:, cols], dims, preferred_element_type=F4)
        out[:, 0:64, :] = part_up.reshape(8, 64, 512).astype(out.dtype)
        part_down = lax.dot_general(dy[...], hid[:, cols], dims, preferred_element_type=F4)
        out[:, 64:128, :] = part_down.reshape(8, 64, 512).astype(out.dtype)
        half = jnp.where(which == 0, gains[:, :256], gains[:, 256:])
        block = jnp.broadcast_to(jnp.concatenate([half, half], axis=1), (16, 512))
        for q in range(8):
            out[q, 128:144, :] = block.astype(out.dtype)
    token[...] = jnp.zeros_like(token)


def pieces_kernel(keep, got, *outs):
    d = lax.axis_index("dp")
    for o in range(8):
        outs[o][...] = (keep[d ^ o] + got[d ^ o].astype(F4)).astype(outs[o].dtype)
    outs[8][...] = jnp.zeros_like(outs[8])


def total_kernel(sofar, *refs):
    *arrived, total, token = refs
    acc = sofar[...]
    for ref in arrived:
        acc = acc + ref[...].astype(F4)
    total[...] = acc
    token[...] = jnp.zeros_like(token)


def choose_kernel(first, second, own, away):
    pair, _ = where_am_i()

    @pl.when(pair < 8)
    def _():
        own[...] = first[...]
        away[...] = second[...].astype(BF)

    @pl.when(pair >= 8)
    def _():
        own[...] = second[...]
        away[...] = first[...].astype(BF)


def finish_kernel(own, got, up, down, gain):
    d = lax.axis_index("dp")
    up[...] = own[0:64, :] + got[0:64, :].astype(F4)
    down[...] = (own[64:128, :] + got[64:128, :].astype(F4)).T
    row = (own[128:144, :] + got[128:144, :].astype(F4))[0:1, :256]
    acc = jnp.zeros((1, 32), F4)
    for q in range(8):
        acc = acc + jnp.where(d == q, row[:, q * 32 : (q + 1) * 32], 0.0)
    gain[...] = acc


PATH = (0, 1, 13, 12, 4, 5, 9, 8)


def hop(block, a, b, spare):
    a, b, spare = PATH[a], PATH[b], PATH[spare]
    route = {}
    for p, q in ((a, b), (b, spare), (spare, a)):
        for c in (0, 1):
            route[2 * p + c] = 2 * q + 1 - c
            route[2 * (15 - p) + c] = 2 * (15 - q) + 1 - c
    return lax.ppermute(block, "segment", [(i, route.get(i, i ^ 1)) for i in range(32)])


def exchange(block):
    return lax.ppermute(block, "segment", [(i, i ^ 1) for i in range(32)])


def low(section):
    return min(section, 15 - section)


def body(feed_rising, feed_falling, up, down, gain):
    width, hidden = up.shape[1], up.shape[2]
    rows = feed_rising.shape[0] * feed_rising.shape[1] // 2
    scale = 1.0 / math.sqrt(2.0 * feed_rising.shape[0] * feed_rising.shape[1] * lax.axis_size("dp"))
    kept = [((rows, width), F4), ((rows, 128), F4), ((rows, width), BF), ((rows, hidden), F4), ((rows, hidden), BF)]
    made = [((rows, hidden), BF), ((rows, width), BF), ((8, width), F4)]
    note = [((8, 128), F4)]

    def nothing(*refs):
        pass

    x, up, down, gain = call(
        load_kernel,
        [((rows, width), BF), (up.shape, BF), (down.shape, BF), (gain.shape, F4)],
        [feed_rising, feed_falling, up, down, gain],
        "load",
        anywhere=True,
        scratch=[pltpu.SemaphoreType.DMA((9,))],
    )
    fresh = call(nothing, (kept + made) * 2 + note, [], "room")
    state = [list(fresh[:5]), list(fresh[8:13])]
    outs = [list(fresh[5:8]), list(fresh[13:16])]
    token = fresh[16]

    def remember(t, x, y):
        which = t // 8
        *state[which], made_note = call(
            lambda *r: keep_kernel(t, *r),
            kept + note,
            [x, up, gain, y, *state[which]],
            f"keep_{t}",
            {4 + i: i for i in range(5)},
            flops=1 << 28,
        )
        return made_note

    pending = None
    for t in range(16):
        y, = call(lambda *r: forward_kernel(t, *r), [((rows, width), BF)], [x, up, down, gain, token], f"fwd_{t}")
        if t == 7:
            pending = (t, x, y)
            x = y
            continue
        new = y
        if t < 15:
            new = hop(y, low(t), low(t + 1), (low(t) + 4) % 8)
        if pending is not None:
            remember(*pending)
            pending = None
        token = remember(t, x, y)
        if t == 1:
            up_t, token = call(transpose_kernel, [((2, hidden, width), BF)] + note, [up, token], "up_t", flops=1 << 28)
        if t == 2:
            down_t, token = call(transpose_kernel, [((2, width, hidden), BF)] + note, [down, token], "down_t", flops=1 << 28)
        x = new

    size = (8, 2 * width // 8 + 16, hidden // 2)

    def grads(which, anchor):
        nb, hid = state[which][2], state[which][4]
        da, dy, gsum = outs[which]
        return call(
            grads_kernel, [(size, F4), (size, BF)] + note, [nb, da, dy, hid, gsum, anchor], f"grads_{which}", flops=1 << 28
        )

    def pieces(which, keep, got):
        *parts, made_note = call(
            pieces_kernel, [(size[1:], F4)] + [(size[1:], BF)] * 7 + note, [keep, got], f"pieces_{which}", flops=1 << 26
        )
        return parts, made_note

    def total(which, sofar, parts, offsets):
        arrived = [lax.ppermute(parts[o], "dp", [(i, i ^ o) for i in range(8)]) for o in offsets]
        return call(
            total_kernel, [(size[1:], F4)] + note, [sofar, *arrived], f"total_{which}_{offsets[0]}", flops=1 << 26
        )

    cot = x
    for s in range(15, -1, -1):
        which = s // 8
        xh, inv, nb, slope, hid = state[which]
        cot_new, *outs[which] = call(
            lambda *r: backward_kernel(s, scale if s == 15 else None, *r),
            [((rows, width), BF)] + made,
            [cot, up_t, down_t, gain, xh, inv, slope, token, *outs[which]],
            f"bwd_{s}",
            {8 + i: 1 + i for i in range(3)},
        )
        cot = cot_new
        if s != 8 and s > 0:
            spare = (low(s) + 4) % 8 if s > 8 else (0, 4, 5, 6, 7, 0, 1, 0)[s]
            cot = hop(cot_new, low(s), low(s - 1), spare)
        if s == 7:
            keep, give, token = grads(1, cot_new)
            got = exchange(give)
        if s == 6:
            parts, token = pieces(1, keep, got)
            second = parts[0]
        if 2 <= s <= 5:
            second, token = total(1, second, parts, {5: (1, 2), 4: (3, 4), 3: (5, 6), 2: (7,)}[s])
    keep, give, _ = grads(0, cot)
    parts, _ = pieces(0, keep, exchange(give))
    first, _ = total(0, parts[0], parts, range(1, 8))
    own, away = call(choose_kernel, [(size[1:], F4), (size[1:], BF)], [first, second], "choose")
    got = lax.ppermute(away, "segment", [(i, (15 - i // 2) * 2 + i % 2) for i in range(32)])
    return call(
        finish_kernel,
        [((width // 8, hidden // 2), F4), ((hidden // 2, width // 8), F4), ((1, width // 16), F4)],
        [own, got],
        "finish",
        plain=True,
    )


def solution(mesh):
    return jax.shard_map(
        lambda *a: tuple(body(*a)),
        mesh=mesh,
        in_specs=(
            P(None, "dp", None),
            P(None, "dp", None),
            P("segment", None, None),
            P("segment", None, None),
            P("segment", None),
        ),
        out_specs=(P("dp", "segment"), P("segment", "dp"), P("segment", "dp")),
        check_vma=False,
    )
```

```python
import math

import jax
import jax.numpy as jnp
from jax import lax
from jax.experimental import pallas as pl
from jax.experimental.pallas import tpu as pltpu
from jax.sharding import PartitionSpec as P

GELU_C = 0.7978845608028654
CUBIC = 0.044715
BF = jnp.bfloat16
F4 = jnp.float32
VMEM = pltpu.VMEM


def in_vmem(x):
    return pltpu.with_memory_space_constraint(x, VMEM)


def call(kernel, outs, ins, name, aliases=None, flops=0, plain=False, anywhere=False, scratch=()):
    space = pl.BlockSpec(memory_space=VMEM)
    if plain:
        shapes = [jax.ShapeDtypeStruct(s, d) for s, d in outs]
    else:
        shapes = [VMEM(s, d) for s, d in outs]
    return pl.pallas_call(
        kernel,
        out_shape=shapes,
        in_specs=[pl.BlockSpec(memory_space=pl.ANY) if anywhere else space] * len(ins),
        out_specs=[space] * len(outs),
        name=name,
        input_output_aliases=aliases or {},
        scratch_shapes=list(scratch),
        cost_estimate=pl.CostEstimate(flops=flops, bytes_accessed=1 << 16, transcendentals=0),
        compiler_params=pltpu.CompilerParams(vmem_limit_bytes=16 << 20),
    )(*[pltpu.with_memory_space_constraint(x, pltpu.HBM) if anywhere else in_vmem(x) for x in ins])


def where_am_i():
    place = lax.axis_index("segment")
    return place // 2, place % 2


def norm_of(values):
    centre = jnp.mean(values, axis=-1, keepdims=True)
    spread = values - centre
    inverse = lax.rsqrt(jnp.mean(spread * spread, axis=-1, keepdims=True) + 1e-05)
    return spread * inverse, inverse


def load_kernel(rising, falling, up, down, gain, rows, up_v, down_v, gain_v, sems):
    pair, core = where_am_i()
    count = rising.shape[0]
    size = rows.shape[0] // count
    part = pl.ds(pl.multiple_of(core * size, size), size)
    late = (pair >= 8).astype(jnp.int32)

    def weights(j, k):
        return [
            pltpu.make_async_copy(up.at[j], up_v.at[j], sems.at[k]),
            pltpu.make_async_copy(down.at[j], down_v.at[j], sems.at[k + 1]),
        ]

    def feed(source):
        return [
            pltpu.make_async_copy(source.at[m, part], rows.at[pl.ds(m * size, size)], sems.at[5 + m])
            for m in range(count)
        ]

    first = weights(late, 0)
    second = weights(1 - late, 2)
    gains = pltpu.make_async_copy(gain, gain_v, sems.at[4])

    @pl.when(pair < 8)
    def _():
        for copy in feed(rising):
            copy.start()

    @pl.when(pair >= 8)
    def _():
        for copy in feed(falling):
            copy.start()

    gains.start()
    for copy in first + second:
        copy.start()
    for copy in feed(rising):
        copy.wait()
    gains.wait()
    for copy in first + second:
        copy.wait()


def transpose_kernel(source, _, out, token):
    for j in range(2):
        out[j] = source[j].T
    token[...] = jnp.zeros_like(token)


def held(section):
    pair, _ = where_am_i()
    late = (pair >= 8).astype(jnp.int32)
    return (pair == section) | (pair == 15 - section), (late if section < 8 else 1 - late)


def forward_kernel(section, rows, up, down, gain, _, emitted):
    turn, j = held(section)

    @pl.when(turn)
    def _():
        values = rows[...].astype(F4)
        normed, _ = norm_of(values)
        normed_b = (normed * gain[pl.ds(j, 1), :]).astype(BF)
        a = jnp.dot(normed_b, up[j], preferred_element_type=F4)
        tangent = jnp.tanh(a * (GELU_C + GELU_C * CUBIC * a * a))
        hidden = (0.5 * a * (1.0 + tangent)).astype(BF)
        emitted[...] = (values + jnp.dot(hidden, down[j], preferred_element_type=F4)).astype(BF)


def keep_kernel(section, rows, up, gain, _y, _a, _b, _c, _d, _e, xh, inv, nb, slope, hid, token):
    turn, j = held(section)

    @pl.when(turn)
    def _():
        normed, inverse = norm_of(rows[...].astype(F4))
        normed_b = (normed * gain[pl.ds(j, 1), :]).astype(BF)
        a = jnp.dot(normed_b, up[j], preferred_element_type=F4)
        square = a * a
        tangent = jnp.tanh(a * (GELU_C + GELU_C * CUBIC * square))
        half = 0.5 * (1.0 + tangent)
        hid[...] = (a * half).astype(BF)
        slope[...] = half + 0.5 * a * (1.0 - tangent * tangent) * (
            GELU_C + 3.0 * GELU_C * CUBIC * square
        )
        xh[...] = normed
        inv[...] = jnp.broadcast_to(inverse, inv.shape)
        nb[...] = normed_b

    token[...] = jnp.zeros_like(token)


def backward_kernel(section, scale, cot, up_t, down_t, gain, xh, inv, slope, _t, _a, _b, _c, sent, da, dy, gsum):
    turn, j = held(section)

    @pl.when(turn)
    def _():
        dy_b = cot[...]
        if scale is not None:
            dy_b = (dy_b.astype(F4) * scale).astype(BF)
        dp = jnp.dot(dy_b, down_t[j], preferred_element_type=F4)
        da_b = (dp * slope[...]).astype(BF)
        dn = jnp.dot(da_b, up_t[j], preferred_element_type=F4)
        normed = xh[...]
        e = dn * gain[pl.ds(j, 1), :]
        first = jnp.mean(e, axis=-1, keepdims=True)
        second = jnp.mean(e * normed, axis=-1, keepdims=True)
        sent[...] = (dy_b.astype(F4) + inv[:, :1] * (e - first - normed * second)).astype(BF)
        da[...] = da_b
        dy[...] = dy_b
        prod = dn * normed
        gsum[...] = jnp.sum(prod.reshape(prod.shape[0] // 8, 8, prod.shape[1]), axis=0)


def grads_kernel(nb, da, dy, hid, gsum, _, keep, give, token):
    _, core = where_am_i()
    dims = (((0,), (0,)), ((), ()))
    gains = jnp.sum(gsum[...], axis=0, keepdims=True)
    for which, out in ((core, keep), (1 - core, give)):
        cols = pl.ds(pl.multiple_of(which * 512, 512), 512)
        part_up = lax.dot_general(nb[...], da[:, cols], dims, preferred_element_type=F4)
        out[:, 0:64, :] = part_up.reshape(8, 64, 512).astype(out.dtype)
        part_down = lax.dot_general(dy[...], hid[:, cols], dims, preferred_element_type=F4)
        out[:, 64:128, :] = part_down.reshape(8, 64, 512).astype(out.dtype)
        half = jnp.where(which == 0, gains[:, :256], gains[:, 256:])
        block = jnp.broadcast_to(jnp.concatenate([half, half], axis=1), (16, 512))
        for q in range(8):
            out[q, 128:144, :] = block.astype(out.dtype)
    token[...] = jnp.zeros_like(token)


def pieces_kernel(keep, got, *outs):
    d = lax.axis_index("dp")
    for o in range(8):
        outs[o][...] = (keep[d ^ o] + got[d ^ o].astype(F4)).astype(outs[o].dtype)
    outs[8][...] = jnp.zeros_like(outs[8])


def total_kernel(sofar, *refs):
    *arrived, total, token = refs
    acc = sofar[...]
    for ref in arrived:
        acc = acc + ref[...].astype(F4)
    total[...] = acc
    token[...] = jnp.zeros_like(token)


def choose_kernel(first, second, own, away):
    pair, _ = where_am_i()

    @pl.when(pair < 8)
    def _():
        own[...] = first[...]
        away[...] = second[...].astype(BF)

    @pl.when(pair >= 8)
    def _():
        own[...] = second[...]
        away[...] = first[...].astype(BF)


def finish_kernel(own, got, up, down, gain):
    d = lax.axis_index("dp")
    up[...] = own[0:64, :] + got[0:64, :].astype(F4)
    down[...] = (own[64:128, :] + got[64:128, :].astype(F4)).T
    row = (own[128:144, :] + got[128:144, :].astype(F4))[0:1, :256]
    acc = jnp.zeros((1, 32), F4)
    for q in range(8):
        acc = acc + jnp.where(d == q, row[:, q * 32 : (q + 1) * 32], 0.0)
    gain[...] = acc


PATH = (0, 1, 13, 12, 4, 5, 9, 8)


def hop(block, a, b, spare):
    a, b, spare = PATH[a], PATH[b], PATH[spare]
    route = {}
    for p, q in ((a, b), (b, spare), (spare, a)):
        for c in (0, 1):
            route[2 * p + c] = 2 * q + c
            route[2 * (15 - p) + c] = 2 * (15 - q) + c
    return lax.ppermute(block, "segment", [(i, route.get(i, i ^ 1)) for i in range(32)])


def exchange(block):
    return lax.ppermute(block, "segment", [(i, i ^ 1) for i in range(32)])


def low(section):
    return min(section, 15 - section)


def body(feed_rising, feed_falling, up, down, gain):
    width, hidden = up.shape[1], up.shape[2]
    rows = feed_rising.shape[0] * feed_rising.shape[1] // 2
    scale = 1.0 / math.sqrt(2.0 * feed_rising.shape[0] * feed_rising.shape[1] * lax.axis_size("dp"))
    kept = [((rows, width), F4), ((rows, 128), F4), ((rows, width), BF), ((rows, hidden), F4), ((rows, hidden), BF)]
    made = [((rows, hidden), BF), ((rows, width), BF), ((8, width), F4)]
    note = [((8, 128), F4)]

    def nothing(*refs):
        pass

    x, up, down, gain = call(
        load_kernel,
        [((rows, width), BF), (up.shape, BF), (down.shape, BF), (gain.shape, F4)],
        [feed_rising, feed_falling, up, down, gain],
        "load",
        anywhere=True,
        scratch=[pltpu.SemaphoreType.DMA((9,))],
    )
    fresh = call(nothing, (kept + made) * 2 + note, [], "room")
    state = [list(fresh[:5]), list(fresh[8:13])]
    outs = [list(fresh[5:8]), list(fresh[13:16])]
    token = fresh[16]

    def remember(t, x, y):
        which = t // 8
        *state[which], made_note = call(
            lambda *r: keep_kernel(t, *r),
            kept + note,
            [x, up, gain, y, *state[which]],
            f"keep_{t}",
            {4 + i: i for i in range(5)},
            flops=1 << 28,
        )
        return made_note

    pending = None
    for t in range(16):
        y, = call(lambda *r: forward_kernel(t, *r), [((rows, width), BF)], [x, up, down, gain, token], f"fwd_{t}")
        if t == 7:
            pending = (t, x, y)
            x = y
            continue
        new = y
        if t < 15:
            new = hop(y, low(t), low(t + 1), (low(t) + 4) % 8)
        if pending is not None:
            remember(*pending)
            pending = None
        token = remember(t, x, y)
        if t == 1:
            up_t, token = call(transpose_kernel, [((2, hidden, width), BF)] + note, [up, token], "up_t", flops=1 << 28)
        if t == 2:
            down_t, token = call(transpose_kernel, [((2, width, hidden), BF)] + note, [down, token], "down_t", flops=1 << 28)
        x = new

    size = (8, 2 * width // 8 + 16, hidden // 2)

    def grads(which, anchor):
        nb, hid = state[which][2], state[which][4]
        da, dy, gsum = outs[which]
        return call(
            grads_kernel, [(size, F4), (size, BF)] + note, [nb, da, dy, hid, gsum, anchor], f"grads_{which}", flops=1 << 28
        )

    def pieces(which, keep, got):
        *parts, made_note = call(
            pieces_kernel, [(size[1:], F4)] + [(size[1:], BF)] * 7 + note, [keep, got], f"pieces_{which}", flops=1 << 26
        )
        return parts, made_note

    def total(which, sofar, parts, offsets):
        arrived = [lax.ppermute(parts[o], "dp", [(i, i ^ o) for i in range(8)]) for o in offsets]
        return call(
            total_kernel, [(size[1:], F4)] + note, [sofar, *arrived], f"total_{which}_{offsets[0]}", flops=1 << 26
        )

    cot = x
    for s in range(15, -1, -1):
        which = s // 8
        xh, inv, nb, slope, hid = state[which]
        cot_new, *outs[which] = call(
            lambda *r: backward_kernel(s, scale if s == 15 else None, *r),
            [((rows, width), BF)] + made,
            [cot, up_t, down_t, gain, xh, inv, slope, token, *outs[which]],
            f"bwd_{s}",
            {8 + i: 1 + i for i in range(3)},
        )
        cot = cot_new
        if s != 8 and s > 0:
            spare = (low(s) + 4) % 8 if s > 8 else (0, 4, 5, 6, 7, 0, 1, 0)[s]
            cot = hop(cot_new, low(s), low(s - 1), spare)
        if s == 7:
            keep, give, token = grads(1, cot_new)
            got = exchange(give)
        if s == 6:
            parts, token = pieces(1, keep, got)
            second = parts[0]
        if 2 <= s <= 5:
            second, token = total(1, second, parts, {5: (1, 2), 4: (3, 4), 3: (5, 6), 2: (7,)}[s])
    keep, give, _ = grads(0, cot)
    parts, _ = pieces(0, keep, exchange(give))
    first, _ = total(0, parts[0], parts, range(1, 8))
    own, away = call(choose_kernel, [(size[1:], F4), (size[1:], BF)], [first, second], "choose")
    got = lax.ppermute(away, "segment", [(i, (15 - i // 2) * 2 + i % 2) for i in range(32)])
    return call(
        finish_kernel,
        [((width // 8, hidden // 2), F4), ((hidden // 2, width // 8), F4), ((1, width // 16), F4)],
        [own, got],
        "finish",
        plain=True,
    )


def solution(mesh):
    return jax.shard_map(
        lambda *a: tuple(body(*a)),
        mesh=mesh,
        in_specs=(
            P(None, "dp", None),
            P(None, "dp", None),
            P("segment", None, None),
            P("segment", None, None),
            P("segment", None),
        ),
        out_specs=(P("dp", "segment"), P("segment", "dp"), P("segment", "dp")),
        check_vma=False,
    )
```

```python
import math

import jax
import jax.numpy as jnp
from jax import lax
from jax.experimental import pallas as pl
from jax.experimental.pallas import tpu as pltpu
from jax.sharding import PartitionSpec as P

GELU_C = 0.7978845608028654
CUBIC = 0.044715
BF = jnp.bfloat16
F4 = jnp.float32
VMEM = pltpu.VMEM
CHUNKS = 2


def in_vmem(x):
    return pltpu.with_memory_space_constraint(x, VMEM)


def call(kernel, outs, ins, name, aliases=None, flops=0, plain=False, anywhere=False, scratch=()):
    space = pl.BlockSpec(memory_space=VMEM)
    if plain:
        shapes = [jax.ShapeDtypeStruct(s, d) for s, d in outs]
    else:
        shapes = [VMEM(s, d) for s, d in outs]
    return pl.pallas_call(
        kernel,
        out_shape=shapes,
        in_specs=[pl.BlockSpec(memory_space=pl.ANY) if anywhere else space] * len(ins),
        out_specs=[space] * len(outs),
        name=name,
        input_output_aliases=aliases or {},
        scratch_shapes=list(scratch),
        cost_estimate=pl.CostEstimate(flops=flops, bytes_accessed=1 << 16, transcendentals=0),
        compiler_params=pltpu.CompilerParams(vmem_limit_bytes=16 << 20),
    )(*[pltpu.with_memory_space_constraint(x, pltpu.HBM) if anywhere else in_vmem(x) for x in ins])


def where_am_i():
    place = lax.axis_index("segment")
    return place // 2, place % 2


def norm_of(values):
    centre = jnp.mean(values, axis=-1, keepdims=True)
    spread = values - centre
    inverse = lax.rsqrt(jnp.mean(spread * spread, axis=-1, keepdims=True) + 1e-05)
    return spread * inverse, inverse


def load_kernel(rising, falling, up, down, gain, rows_a, rows_b, up_v, down_v, gain_v, sems):
    pair, core = where_am_i()
    count = rising.shape[0]
    each = count // CHUNKS
    size = rows_a.shape[0] // each
    part = pl.ds(pl.multiple_of(core * size, size), size)
    late = (pair >= 8).astype(jnp.int32)

    def weights(j, k):
        return [
            pltpu.make_async_copy(up.at[j], up_v.at[j], sems.at[k]),
            pltpu.make_async_copy(down.at[j], down_v.at[j], sems.at[k + 1]),
        ]

    def feed(source):
        return [
            pltpu.make_async_copy(
                source.at[m, part], (rows_a, rows_b)[m // each].at[pl.ds(m % each * size, size)], sems.at[5 + m]
            )
            for m in range(count)
        ]

    first = weights(late, 0)
    second = weights(1 - late, 2)
    gains = pltpu.make_async_copy(gain, gain_v, sems.at[4])

    @pl.when(pair < 8)
    def _():
        for copy in feed(rising):
            copy.start()

    @pl.when(pair >= 8)
    def _():
        for copy in feed(falling):
            copy.start()

    gains.start()
    for copy in first + second:
        copy.start()
    for copy in feed(rising):
        copy.wait()
    gains.wait()
    for copy in first + second:
        copy.wait()


def transpose_kernel(source, _, out, token):
    for j in range(2):
        out[j] = source[j].T
    token[...] = jnp.zeros_like(token)


def held(section):
    pair, _ = where_am_i()
    late = (pair >= 8).astype(jnp.int32)
    return (pair == section) | (pair == 15 - section), (late if section < 8 else 1 - late)


def forward_kernel(section, rows, up, down, gain, _, emitted):
    turn, j = held(section)

    @pl.when(turn)
    def _():
        values = rows[...].astype(F4)
        normed, _ = norm_of(values)
        normed_b = (normed * gain[pl.ds(j, 1), :]).astype(BF)
        a = jnp.dot(normed_b, up[j], preferred_element_type=F4)
        tangent = jnp.tanh(a * (GELU_C + GELU_C * CUBIC * a * a))
        hidden = (0.5 * a * (1.0 + tangent)).astype(BF)
        emitted[...] = (values + jnp.dot(hidden, down[j], preferred_element_type=F4)).astype(BF)


def keep_kernel(section, rows_a, rows_b, up, gain, _y, _z, _a, _b, _c, _d, _e, xh, inv, nb, slope, hid, token):
    turn, j = held(section)

    @pl.when(turn)
    def _():
        normed, inverse = norm_of(jnp.concatenate([rows_a[...], rows_b[...]], axis=0).astype(F4))
        normed_b = (normed * gain[pl.ds(j, 1), :]).astype(BF)
        a = jnp.dot(normed_b, up[j], preferred_element_type=F4)
        square = a * a
        tangent = jnp.tanh(a * (GELU_C + GELU_C * CUBIC * square))
        half = 0.5 * (1.0 + tangent)
        hid[...] = (a * half).astype(BF)
        slope[...] = half + 0.5 * a * (1.0 - tangent * tangent) * (
            GELU_C + 3.0 * GELU_C * CUBIC * square
        )
        xh[...] = normed
        inv[...] = jnp.broadcast_to(inverse, inv.shape)
        nb[...] = normed_b

    token[...] = jnp.zeros_like(token)


def backward_kernel(section, scale, chunk, cot, up_t, down_t, gain, xh, inv, slope, _t, _a, _b, _c, sent, da, dy, gsum):
    turn, j = held(section)
    part = slice(chunk * cot.shape[0], (chunk + 1) * cot.shape[0])

    @pl.when(turn)
    def _():
        dy_b = cot[...]
        if scale is not None:
            dy_b = (dy_b.astype(F4) * scale).astype(BF)
        dp = jnp.dot(dy_b, down_t[j], preferred_element_type=F4)
        da_b = (dp * slope[part, :]).astype(BF)
        dn = jnp.dot(da_b, up_t[j], preferred_element_type=F4)
        normed = xh[part, :]
        e = dn * gain[pl.ds(j, 1), :]
        first = jnp.mean(e, axis=-1, keepdims=True)
        second = jnp.mean(e * normed, axis=-1, keepdims=True)
        sent[...] = (dy_b.astype(F4) + inv[part, :1] * (e - first - normed * second)).astype(BF)
        da[part, :] = da_b
        dy[part, :] = dy_b
        prod = dn * normed
        gsum[8 * chunk : 8 * chunk + 8, :] = jnp.sum(prod.reshape(prod.shape[0] // 8, 8, prod.shape[1]), axis=0)


def grads_kernel(nb, da, dy, hid, gsum, _, keep, give, token):
    _, core = where_am_i()
    dims = (((0,), (0,)), ((), ()))
    gains = jnp.sum(gsum[...], axis=0, keepdims=True)
    for which, out in ((core, keep), (1 - core, give)):
        cols = pl.ds(pl.multiple_of(which * 512, 512), 512)
        part_up = lax.dot_general(nb[...], da[:, cols], dims, preferred_element_type=F4)
        out[:, 0:64, :] = part_up.reshape(8, 64, 512).astype(out.dtype)
        part_down = lax.dot_general(dy[...], hid[:, cols], dims, preferred_element_type=F4)
        out[:, 64:128, :] = part_down.reshape(8, 64, 512).astype(out.dtype)
        half = jnp.where(which == 0, gains[:, :256], gains[:, 256:])
        block = jnp.broadcast_to(jnp.concatenate([half, half], axis=1), (16, 512))
        for q in range(8):
            out[q, 128:144, :] = block.astype(out.dtype)
    token[...] = jnp.zeros_like(token)


def pieces_kernel(keep, got, *outs):
    d = lax.axis_index("dp")
    for o in range(8):
        outs[o][...] = (keep[d ^ o] + got[d ^ o].astype(F4)).astype(outs[o].dtype)
    outs[8][...] = jnp.zeros_like(outs[8])


def total_kernel(sofar, *refs):
    *arrived, total, token = refs
    acc = sofar[...]
    for ref in arrived:
        acc = acc + ref[...].astype(F4)
    total[...] = acc
    token[...] = jnp.zeros_like(token)


def choose_kernel(first, second, own, away):
    pair, _ = where_am_i()

    @pl.when(pair < 8)
    def _():
        own[...] = first[...]
        away[...] = second[...].astype(BF)

    @pl.when(pair >= 8)
    def _():
        own[...] = second[...]
        away[...] = first[...].astype(BF)


def finish_kernel(own, got, up, down, gain):
    d = lax.axis_index("dp")
    up[...] = own[0:64, :] + got[0:64, :].astype(F4)
    down[...] = (own[64:128, :] + got[64:128, :].astype(F4)).T
    row = (own[128:144, :] + got[128:144, :].astype(F4))[0:1, :256]
    acc = jnp.zeros((1, 32), F4)
    for q in range(8):
        acc = acc + jnp.where(d == q, row[:, q * 32 : (q + 1) * 32], 0.0)
    gain[...] = acc


PATH = (0, 1, 13, 12, 4, 5, 9, 8)


def hop(block, a, b):
    ring = [PATH[a], PATH[b]] + ([] if {a, b} == {6, 7} else [PATH[(a + 4) % 8]])
    route = {}
    for p, q in zip(ring, ring[1:] + ring[:1]):
        for c in (0, 1):
            route[2 * p + c] = 2 * q + c
            route[2 * (15 - p) + c] = 2 * (15 - q) + c
    return lax.ppermute(block, "segment", [(i, route.get(i, i ^ 1)) for i in range(32)])


def exchange(block):
    return lax.ppermute(block, "segment", [(i, i ^ 1) for i in range(32)])


def low(section):
    return min(section, 15 - section)


def body(feed_rising, feed_falling, up, down, gain):
    width, hidden = up.shape[1], up.shape[2]
    rows = feed_rising.shape[0] * feed_rising.shape[1] // 2
    scale = 1.0 / math.sqrt(2.0 * feed_rising.shape[0] * feed_rising.shape[1] * lax.axis_size("dp"))
    kept = [((rows, width), F4), ((rows, 128), F4), ((rows, width), BF), ((rows, hidden), F4), ((rows, hidden), BF)]
    made = [((rows, hidden), BF), ((rows, width), BF), ((8 * CHUNKS, width), F4)]
    block = [((rows // CHUNKS, width), BF)]
    note = [((8, 128), F4)]

    def nothing(*refs):
        pass

    *x, up, down, gain = call(
        load_kernel,
        [*block * CHUNKS, (up.shape, BF), (down.shape, BF), (gain.shape, F4)],
        [feed_rising, feed_falling, up, down, gain],
        "load",
        anywhere=True,
        scratch=[pltpu.SemaphoreType.DMA((9,))],
    )
    fresh = call(nothing, (kept + made) * 2 + note, [], "room")
    state = [list(fresh[:5]), list(fresh[8:13])]
    outs = [list(fresh[5:8]), list(fresh[13:16])]
    token = fresh[16]

    def remember(t, x, y):
        which = t // 8
        *state[which], made_note = call(
            lambda *r: keep_kernel(t, *r),
            kept + note,
            [*x, up, gain, *y, *state[which]],
            f"keep_{t}",
            {6 + i: i for i in range(5)},
            flops=1 << 28,
        )
        return made_note

    pending = None
    for t in range(16):
        y, new = [], []
        for c in range(CHUNKS):
            made_rows, = call(lambda *r: forward_kernel(t, *r), block, [x[c], up, down, gain, token], f"fwd_{t}_{c}")
            y.append(made_rows)
            moves = t != 7 and t < 15
            new.append(hop(made_rows, low(t), low(t + 1)) if moves else made_rows)
        if t == 7:
            pending = (t, x, y)
            x = y
            continue
        if pending is not None:
            remember(*pending)
            pending = None
        token = remember(t, x, y)
        if t == 1:
            up_t, token = call(transpose_kernel, [((2, hidden, width), BF)] + note, [up, token], "up_t", flops=1 << 28)
        if t == 2:
            down_t, token = call(transpose_kernel, [((2, width, hidden), BF)] + note, [down, token], "down_t", flops=1 << 28)
        x = new

    size = (8, 2 * width // 8 + 16, hidden // 2)

    def grads(which, anchor):
        nb, hid = state[which][2], state[which][4]
        da, dy, gsum = outs[which]
        return call(
            grads_kernel, [(size, F4), (size, BF)] + note, [nb, da, dy, hid, gsum, anchor], f"grads_{which}", flops=1 << 28
        )

    def pieces(which, keep, got):
        *parts, made_note = call(
            pieces_kernel, [(size[1:], F4)] + [(size[1:], BF)] * 7 + note, [keep, got], f"pieces_{which}", flops=1 << 26
        )
        return parts, made_note

    def total(which, sofar, parts, offsets):
        arrived = [lax.ppermute(parts[o], "dp", [(i, i ^ o) for i in range(8)]) for o in offsets]
        return call(
            total_kernel, [(size[1:], F4)] + note, [sofar, *arrived], f"total_{which}_{offsets[0]}", flops=1 << 26
        )

    cot = x
    for s in range(15, -1, -1):
        which = s // 8
        xh, inv, nb, slope, hid = state[which]
        sent = []
        for c in range(CHUNKS):
            cot_new, *outs[which] = call(
                lambda *r: backward_kernel(s, scale if s == 15 else None, c, *r),
                block + made,
                [cot[c], up_t, down_t, gain, xh, inv, slope, token, *outs[which]],
                f"bwd_{s}_{c}",
                {8 + i: 1 + i for i in range(3)},
            )
            if s != 8 and s > 0:
                sent.append(hop(cot_new, low(s), low(s - 1)))
            else:
                sent.append(cot_new)
        cot = sent
        if s == 6:
            keep, give, token = grads(1, cot_new)
            got = exchange(give)
        if s == 5:
            parts, _ = pieces(1, keep, got)
            second = parts[0]
        if 2 <= s <= 5:
            second, token = total(1, second, parts, {5: (1, 2), 4: (3, 4), 3: (5, 6), 2: (7,)}[s])
    keep, give, _ = grads(0, cot[-1])
    parts, _ = pieces(0, keep, exchange(give))
    first, _ = total(0, parts[0], parts, range(1, 8))
    own, away = call(choose_kernel, [(size[1:], F4), (size[1:], BF)], [first, second], "choose")
    got = lax.ppermute(away, "segment", [(i, (15 - i // 2) * 2 + i % 2) for i in range(32)])
    return call(
        finish_kernel,
        [((width // 8, hidden // 2), F4), ((hidden // 2, width // 8), F4), ((1, width // 16), F4)],
        [own, got],
        "finish",
        plain=True,
    )


def solution(mesh):
    return jax.shard_map(
        lambda *a: tuple(body(*a)),
        mesh=mesh,
        in_specs=(
            P(None, "dp", None),
            P(None, "dp", None),
            P("segment", None, None),
            P("segment", None, None),
            P("segment", None),
        ),
        out_specs=(P("dp", "segment"), P("segment", "dp"), P("segment", "dp")),
        check_vma=False,
    )
```

```python
import math

import jax
import jax.numpy as jnp
from jax import lax
from jax.experimental import pallas as pl
from jax.experimental.pallas import tpu as pltpu
from jax.sharding import PartitionSpec as P

GELU_C = 0.7978845608028654
CUBIC = 0.044715
BF = jnp.bfloat16
F4 = jnp.float32
VMEM = pltpu.VMEM
CHUNKS = 2


def in_vmem(x):
    return pltpu.with_memory_space_constraint(x, VMEM)


def call(kernel, outs, ins, name, aliases=None, flops=0, plain=False, anywhere=False, scratch=()):
    space = pl.BlockSpec(memory_space=VMEM)
    if plain:
        shapes = [jax.ShapeDtypeStruct(s, d) for s, d in outs]
    else:
        shapes = [VMEM(s, d) for s, d in outs]
    return pl.pallas_call(
        kernel,
        out_shape=shapes,
        in_specs=[pl.BlockSpec(memory_space=pl.ANY) if anywhere else space] * len(ins),
        out_specs=[space] * len(outs),
        name=name,
        input_output_aliases=aliases or {},
        scratch_shapes=list(scratch),
        cost_estimate=pl.CostEstimate(flops=flops, bytes_accessed=1 << 16, transcendentals=0),
        compiler_params=pltpu.CompilerParams(vmem_limit_bytes=16 << 20),
    )(*[pltpu.with_memory_space_constraint(x, pltpu.HBM) if anywhere else in_vmem(x) for x in ins])


def where_am_i():
    place = lax.axis_index("segment")
    return place // 2, place % 2


def norm_of(values):
    centre = jnp.mean(values, axis=-1, keepdims=True)
    spread = values - centre
    inverse = lax.rsqrt(jnp.mean(spread * spread, axis=-1, keepdims=True) + 1e-05)
    return spread * inverse, inverse


def load_kernel(rising, falling, up, down, gain, rows_a, rows_b, up_v, down_v, gain_v, sems):
    pair, core = where_am_i()
    count = rising.shape[0]
    each = count // CHUNKS
    size = rows_a.shape[0] // each
    part = pl.ds(pl.multiple_of(core * size, size), size)
    late = (pair >= 8).astype(jnp.int32)

    def weights(j, k):
        return [
            pltpu.make_async_copy(up.at[j], up_v.at[j], sems.at[k]),
            pltpu.make_async_copy(down.at[j], down_v.at[j], sems.at[k + 1]),
        ]

    def feed(source):
        return [
            pltpu.make_async_copy(
                source.at[m, part], (rows_a, rows_b)[m // each].at[pl.ds(m % each * size, size)], sems.at[5 + m]
            )
            for m in range(count)
        ]

    first = weights(late, 0)
    second = weights(1 - late, 2)
    gains = pltpu.make_async_copy(gain, gain_v, sems.at[4])

    @pl.when(pair < 8)
    def _():
        for copy in feed(rising):
            copy.start()

    @pl.when(pair >= 8)
    def _():
        for copy in feed(falling):
            copy.start()

    gains.start()
    for copy in first + second:
        copy.start()
    for copy in feed(rising):
        copy.wait()
    gains.wait()
    for copy in first + second:
        copy.wait()


def transpose_kernel(source, _, out, token):
    for j in range(2):
        out[j] = source[j].T
    token[...] = jnp.zeros_like(token)


def held(section):
    pair, _ = where_am_i()
    late = (pair >= 8).astype(jnp.int32)
    return (pair == section) | (pair == 15 - section), (late if section < 8 else 1 - late)


def forward_kernel(section, rows, up, down, gain, _, emitted):
    turn, j = held(section)

    @pl.when(turn)
    def _():
        values = rows[...].astype(F4)
        normed, _ = norm_of(values)
        normed_b = (normed * gain[pl.ds(j, 1), :]).astype(BF)
        a = jnp.dot(normed_b, up[j], preferred_element_type=F4)
        tangent = jnp.tanh(a * (GELU_C + GELU_C * CUBIC * a * a))
        hidden = (0.5 * a * (1.0 + tangent)).astype(BF)
        emitted[...] = (values + jnp.dot(hidden, down[j], preferred_element_type=F4)).astype(BF)


def keep_kernel(section, rows_a, rows_b, up, gain, _y, _z, _a, _b, _c, _d, _e, xh, inv, nb, slope, hid, token):
    turn, j = held(section)

    @pl.when(turn)
    def _():
        normed, inverse = norm_of(jnp.concatenate([rows_a[...], rows_b[...]], axis=0).astype(F4))
        normed_b = (normed * gain[pl.ds(j, 1), :]).astype(BF)
        a = jnp.dot(normed_b, up[j], preferred_element_type=F4)
        square = a * a
        tangent = jnp.tanh(a * (GELU_C + GELU_C * CUBIC * square))
        half = 0.5 * (1.0 + tangent)
        hid[...] = (a * half).astype(BF)
        slope[...] = half + 0.5 * a * (1.0 - tangent * tangent) * (
            GELU_C + 3.0 * GELU_C * CUBIC * square
        )
        xh[...] = normed
        inv[...] = jnp.broadcast_to(inverse, inv.shape)
        nb[...] = normed_b

    token[...] = jnp.zeros_like(token)


def backward_kernel(section, scale, chunk, cot, up_t, down_t, gain, xh, inv, slope, _t, _a, _b, _c, sent, da, dy, gsum):
    turn, j = held(section)
    part = slice(chunk * cot.shape[0], (chunk + 1) * cot.shape[0])

    @pl.when(turn)
    def _():
        dy_b = cot[...]
        if scale is not None:
            dy_b = (dy_b.astype(F4) * scale).astype(BF)
        dp = jnp.dot(dy_b, down_t[j], preferred_element_type=F4)
        da_b = (dp * slope[part, :]).astype(BF)
        dn = jnp.dot(da_b, up_t[j], preferred_element_type=F4)
        normed = xh[part, :]
        e = dn * gain[pl.ds(j, 1), :]
        first = jnp.mean(e, axis=-1, keepdims=True)
        second = jnp.mean(e * normed, axis=-1, keepdims=True)
        sent[...] = (dy_b.astype(F4) + inv[part, :1] * (e - first - normed * second)).astype(BF)
        da[part, :] = da_b
        dy[part, :] = dy_b
        prod = dn * normed
        gsum[8 * chunk : 8 * chunk + 8, :] = jnp.sum(prod.reshape(prod.shape[0] // 8, 8, prod.shape[1]), axis=0)


def grads_kernel(nb, da, dy, hid, gsum, _, keep, give, token):
    _, core = where_am_i()
    dims = (((0,), (0,)), ((), ()))
    gains = jnp.sum(gsum[...], axis=0, keepdims=True)
    for which, out in ((core, keep), (1 - core, give)):
        cols = pl.ds(pl.multiple_of(which * 512, 512), 512)
        part_up = lax.dot_general(nb[...], da[:, cols], dims, preferred_element_type=F4)
        out[:, 0:64, :] = part_up.reshape(8, 64, 512).astype(out.dtype)
        part_down = lax.dot_general(dy[...], hid[:, cols], dims, preferred_element_type=F4)
        out[:, 64:128, :] = part_down.reshape(8, 64, 512).astype(out.dtype)
        half = jnp.where(which == 0, gains[:, :256], gains[:, 256:])
        block = jnp.broadcast_to(jnp.concatenate([half, half], axis=1), (16, 512))
        for q in range(8):
            out[q, 128:144, :] = block.astype(out.dtype)
    token[...] = jnp.zeros_like(token)


def pieces_kernel(keep, got, _, *outs):
    d = lax.axis_index("dp")
    for o in range(8):
        outs[o][...] = (keep[d ^ o] + got[d ^ o].astype(F4)).astype(outs[o].dtype)
    outs[8][...] = jnp.zeros_like(outs[8])


def total_kernel(sofar, *refs):
    *arrived, total, token = refs
    acc = sofar[...]
    for ref in arrived:
        acc = acc + ref[...].astype(F4)
    total[...] = acc
    token[...] = jnp.zeros_like(token)


def choose_kernel(first, second, own, away):
    pair, _ = where_am_i()

    @pl.when(pair < 8)
    def _():
        own[...] = first[...]
        away[...] = second[...].astype(BF)

    @pl.when(pair >= 8)
    def _():
        own[...] = second[...]
        away[...] = first[...].astype(BF)


def finish_kernel(own, got, up, down, gain):
    d = lax.axis_index("dp")
    up[...] = own[0:64, :] + got[0:64, :].astype(F4)
    down[...] = (own[64:128, :] + got[64:128, :].astype(F4)).T
    row = (own[128:144, :] + got[128:144, :].astype(F4))[0:1, :256]
    acc = jnp.zeros((1, 32), F4)
    for q in range(8):
        acc = acc + jnp.where(d == q, row[:, q * 32 : (q + 1) * 32], 0.0)
    gain[...] = acc


PATH = (0, 1, 13, 12, 4, 5, 9, 8)


def hop(block, a, b):
    ring = [PATH[a], PATH[b]] + ([] if {a, b} == {6, 7} else [PATH[(a + 4) % 8]])
    route = {}
    for p, q in zip(ring, ring[1:] + ring[:1]):
        for c in (0, 1):
            route[2 * p + c] = 2 * q + c
            route[2 * (15 - p) + c] = 2 * (15 - q) + c
    return lax.ppermute(block, "segment", [(i, route.get(i, i ^ 1)) for i in range(32)])


def exchange(block):
    return lax.ppermute(block, "segment", [(i, i ^ 1) for i in range(32)])


def low(section):
    return min(section, 15 - section)


def body(feed_rising, feed_falling, up, down, gain):
    width, hidden = up.shape[1], up.shape[2]
    rows = feed_rising.shape[0] * feed_rising.shape[1] // 2
    scale = 1.0 / math.sqrt(2.0 * feed_rising.shape[0] * feed_rising.shape[1] * lax.axis_size("dp"))
    kept = [((rows, width), F4), ((rows, 128), F4), ((rows, width), BF), ((rows, hidden), F4), ((rows, hidden), BF)]
    made = [((rows, hidden), BF), ((rows, width), BF), ((8 * CHUNKS, width), F4)]
    block = [((rows // CHUNKS, width), BF)]
    note = [((8, 128), F4)]

    def nothing(*refs):
        pass

    *x, up, down, gain = call(
        load_kernel,
        [*block * CHUNKS, (up.shape, BF), (down.shape, BF), (gain.shape, F4)],
        [feed_rising, feed_falling, up, down, gain],
        "load",
        anywhere=True,
        scratch=[pltpu.SemaphoreType.DMA((9,))],
    )
    fresh = call(nothing, (kept + made) * 2 + note, [], "room")
    state = [list(fresh[:5]), list(fresh[8:13])]
    outs = [list(fresh[5:8]), list(fresh[13:16])]
    token = fresh[16]

    def remember(t, x, y):
        which = t // 8
        *state[which], made_note = call(
            lambda *r: keep_kernel(t, *r),
            kept + note,
            [*x, up, gain, *y, *state[which]],
            f"keep_{t}",
            {6 + i: i for i in range(5)},
            flops=1 << 28,
        )
        return made_note

    pending = None
    for t in range(16):
        y, new = [], []
        for c in range(CHUNKS):
            made_rows, = call(lambda *r: forward_kernel(t, *r), block, [x[c], up, down, gain, token], f"fwd_{t}_{c}")
            y.append(made_rows)
            moves = t != 7 and t < 15
            new.append(hop(made_rows, low(t), low(t + 1)) if moves else made_rows)
        if t == 7:
            pending = (t, x, y)
            x = y
            continue
        if pending is not None:
            remember(*pending)
            pending = None
        token = remember(t, x, y)
        if t == 1:
            up_t, token = call(transpose_kernel, [((2, hidden, width), BF)] + note, [up, token], "up_t", flops=1 << 28)
        if t == 2:
            down_t, token = call(transpose_kernel, [((2, width, hidden), BF)] + note, [down, token], "down_t", flops=1 << 28)
        x = new

    size = (8, 2 * width // 8 + 16, hidden // 2)

    def grads(which, anchor):
        nb, hid = state[which][2], state[which][4]
        da, dy, gsum = outs[which]
        return call(
            grads_kernel, [(size, F4), (size, BF)] + note, [nb, da, dy, hid, gsum, anchor], f"grads_{which}", flops=1 << 28
        )

    def pieces(which, keep, got, anchor):
        *parts, made_note = call(
            pieces_kernel, [(size[1:], F4)] + [(size[1:], BF)] * 7 + note, [keep, got, anchor], f"pieces_{which}", flops=1 << 26
        )
        return parts, made_note

    def total(which, sofar, parts, offsets):
        arrived = [lax.ppermute(parts[o], "dp", [(i, i ^ o) for i in range(8)]) for o in offsets]
        return call(
            total_kernel, [(size[1:], F4)] + note, [sofar, *arrived], f"total_{which}_{offsets[0]}", flops=1 << 26
        )

    cot = x
    for s in range(15, -1, -1):
        which = s // 8
        xh, inv, nb, slope, hid = state[which]
        sent = []
        for c in range(CHUNKS):
            cot_new, *outs[which] = call(
                lambda *r: backward_kernel(s, scale if s == 15 else None, c, *r),
                block + made,
                [cot[c], up_t, down_t, gain, xh, inv, slope, token, *outs[which]],
                f"bwd_{s}_{c}",
                {8 + i: 1 + i for i in range(3)},
            )
            if s != 8 and s > 0:
                sent.append(hop(cot_new, low(s), low(s - 1)))
            else:
                sent.append(cot_new)
        cot = sent
        if s == 6:
            keep, give, token = grads(1, cot_new)
            got = exchange(give)
            moved = cot[0]
        if s == 5:
            parts, _ = pieces(1, keep, got, moved)
            second = parts[0]
        if 2 <= s <= 5:
            second, token = total(1, second, parts, {5: (1, 2), 4: (3, 4), 3: (5, 6), 2: (7,)}[s])
    keep, give, _ = grads(0, cot[-1])
    parts, _ = pieces(0, keep, exchange(give), cot[0])
    first, _ = total(0, parts[0], parts, range(1, 8))
    own, away = call(choose_kernel, [(size[1:], F4), (size[1:], BF)], [first, second], "choose")
    got = lax.ppermute(away, "segment", [(i, (15 - i // 2) * 2 + i % 2) for i in range(32)])
    return call(
        finish_kernel,
        [((width // 8, hidden // 2), F4), ((hidden // 2, width // 8), F4), ((1, width // 16), F4)],
        [own, got],
        "finish",
        plain=True,
    )


def solution(mesh):
    return jax.shard_map(
        lambda *a: tuple(body(*a)),
        mesh=mesh,
        in_specs=(
            P(None, "dp", None),
            P(None, "dp", None),
            P("segment", None, None),
            P("segment", None, None),
            P("segment", None),
        ),
        out_specs=(P("dp", "segment"), P("segment", "dp"), P("segment", "dp")),
        check_vma=False,
    )
```
